512 devices in a mesh: index: 16 (over z), head: 32 (over x, y, core).
Axes of the slice: x: 4, y: 4, z: 16, core: 2. Of those that a mesh axis runs over, the one named last changes fastest.
Arguments:
- queries: bfloat16 [4096, 4096], P('head'), may hold values from -32 to 32
- local_read: bfloat16 [4096, 4096], P(('index', 'head')), may hold values from -1.5 to 1.5
- gate_logits: float32 [32], replicated, may hold values from -2 to 2
- memory_keys: bfloat16 [16, 32, 4096, 128], P('index', 'head'), may hold values from -32 to 32
- memory_values: bfloat16 [16, 32, 4096, 128], P('index', 'head'), may hold values from -8 to 8
- probe_blocks: int32 [16, 32, 16], P('index', 'head'), may hold values from 0 to 31
- probe_counts: int32 [16, 32], P('index', 'head'), may hold values from 1 to 16, 256 in all within a row
Outputs:
- layer_read: bfloat16 [4096, 4096], P(('index', 'head'))
The draws below stay inside these ranges and needn't reach their ends.
Inputs may be any that keep to these rules, and one draw needn't show every extreme that they name: `probe_counts`: in each group the counts over heads sum to 256.
All inputs are finite; a program needn't handle non-finite values.
Results may differ from the reference program's by a relative error of at most 0.0041.
Values may be sent and summed in bfloat16 or wider, within the bound.
A program may use at most 64 MiB of HBM per device.

```python
import math
import jax
import jax.numpy as jnp
import numpy as np
from jax import lax

DH = 128
BLOCK = 128
PMAX = 16
MEM = 4096
HEADS = 32
GROUPS = 16
D = 4096
TOKENS = 4096
NB = 32


def draw_queries(key, part):
    key = jax.random.fold_in(key, 11)
    values = 3.0 * jax.random.normal(key, (TOKENS, HEADS, DH), jnp.float32)
    values = jnp.clip(values, -32.0, 32.0)
    return values.reshape(TOKENS, HEADS * DH).astype(jnp.bfloat16)


def draw_memory_keys(key, part):
    key = jax.random.fold_in(key, 13)
    values = jax.random.normal(key, (GROUPS, HEADS, MEM, DH), jnp.float32)
    values = jnp.clip(values, -32.0, 32.0)
    return values.astype(jnp.bfloat16)


def draw_memory_values(key, part):
    key = jax.random.fold_in(key, 23)
    values = jnp.clip(jax.random.normal(key, (GROUPS, HEADS, MEM, DH), jnp.float32), -6.0, 6.0)
    return values.astype(jnp.bfloat16)


def draw_gate_logits(key, part):
    key = jax.random.fold_in(key, 29)
    values = jax.random.uniform(key, (HEADS,), jnp.float32, -2.0, 2.0)
    return values


def with_ends(result, own_key, low, largest):
    longest = result.shape.index(max(result.shape))
    spots = []
    for shift in (0, 1):
        where = [jax.random.randint(jax.random.fold_in(own_key, axis), (), 0, length) for axis, length in enumerate(result.shape)]
        where[longest] = (where[longest] + shift) % result.shape[longest]
        spots.append(tuple(where))
    return result.at[spots[0]].set(low).at[spots[1]].set(largest)


def steps_of(stream_key, shape, pieces, low, high):
    factor_of, own = 1.0, jax.random.fold_in(stream_key, 6)
    for position, shards_of in pieces:
        steps = jnp.exp(jax.random.uniform(jax.random.fold_in(own, position), (shards_of,), jnp.float32, low / len(pieces), high / len(pieces)))
        factor_of = factor_of * jnp.repeat(steps, shape[position] // shards_of).reshape([-1 if axis == position else 1 for axis in range(len(shape))])
    return factor_of


def split_up(count, total, most, skew):
    weights = [(1 << 20) // math.isqrt(rank ** skew) + 1 for rank in range(2, count + 1)]
    spare, given = total - most - (count - 1), [1] * (count - 1)
    while spare > 0:
        candidates = [i for i in range(count - 1) if given[i] < most]
        pool, left = sum([weights[i] for i in candidates]), spare
        for i in candidates:
            addition = min(most - given[i], max(1, left * weights[i] // pool), spare)
            given[i] = given[i] + addition
            spare = spare - addition
    return np.array([most] + given)


def uneven(own_key, number_of, total, reach, slope):
    if number_of == 2:
        one = jax.random.randint(own_key, (), max(1, total - reach), min(reach, total - 1) + 1)
        return jnp.stack([one, total - one])
    lengths = jnp.asarray(split_up(number_of, total, reach, slope), jnp.int32)
    couples = (number_of - 1) // 2
    giver, taker = lengths[1:1 + 2 * couples:2], lengths[2:2 + 2 * couples:2]
    margin = jnp.minimum(giver - 1, reach - taker)
    passed = jax.random.randint(jax.random.fold_in(own_key, 1), (couples,), 0, 1 << 20) % (margin + 1)
    lengths = lengths.at[1:1 + 2 * couples:2].set(giver - passed).at[2:2 + 2 * couples:2].set(taker + passed)
    return lengths[jax.random.permutation(jax.random.fold_in(own_key, 2), number_of)]


def gaussian(stream_key, dims, scale, bound, shards=(), held_as=jnp.bfloat16):
    drawn = scale * jax.random.normal(stream_key, dims, jnp.float32)
    if shards:
        drawn = drawn * steps_of(stream_key, dims, shards, -0.22, 0.18)
    return jnp.clip(drawn, -bound, bound).astype(held_as)


def setup_inputs(seed: int = 0) -> dict:
    streams_of = jax.random.split(jax.random.key(seed), 8)
    queries = draw_queries(jax.random.fold_in(streams_of[7], 71), 0)
    local_read = gaussian(streams_of[1], (TOKENS, D), 0.25, 1.5, ((0, 512),))
    gate_logits = draw_gate_logits(jax.random.fold_in(streams_of[7], 71), 0)
    memory_keys = draw_memory_keys(jax.random.fold_in(streams_of[7], 71), 0)
    memory_values = draw_memory_values(jax.random.fold_in(streams_of[7], 71), 0)
    probe_blocks = with_ends(jax.random.randint(streams_of[5], (GROUPS, HEADS, PMAX), 0, NB), jax.random.fold_in(streams_of[5], 1), 0, NB - 1).astype(jnp.int32)
    probe_counts = jax.vmap(lambda own: uneven(own, HEADS, HEADS * PMAX // 2, PMAX, 2))(jax.random.split(streams_of[6], GROUPS)).reshape((GROUPS, HEADS)).astype(jnp.int32)
    return dict(queries=queries, local_read=local_read, gate_logits=gate_logits, memory_keys=memory_keys, memory_values=memory_values, probe_blocks=probe_blocks, probe_counts=probe_counts)


def slab_read(head_queries, key_slab, value_slab, blocks, live_count):
    offsets = jnp.arange(BLOCK, dtype=jnp.int32)
    row_ids = (blocks.astype(jnp.int32)[:, None] * BLOCK + offsets[None, :]).reshape(-1)
    picked_keys = jnp.take(key_slab, row_ids, axis=0)
    picked_values = jnp.take(value_slab, row_ids, axis=0)
    usable = jnp.repeat(jnp.arange(PMAX, dtype=jnp.int32) < live_count, BLOCK)
    scores = jnp.dot(head_queries, picked_keys.T, preferred_element_type=jnp.float32) * (DH ** -0.5)
    scores = jnp.where(usable[None, :], scores, -jnp.inf)
    maxima = jnp.max(scores, axis=1)
    weights = jnp.exp(scores - maxima[:, None])
    totals = jnp.sum(weights, axis=1)
    weighted = jnp.dot(weights.astype(jnp.bfloat16), picked_values, preferred_element_type=jnp.float32)
    return maxima, totals, weighted


def reference(queries, local_read, gate_logits, memory_keys, memory_values, probe_blocks, probe_counts):
    def per_head(head_id):
        head_queries = lax.dynamic_slice_in_dim(queries, head_id * DH, DH, 1)

        def per_group(group_id):
            return slab_read(head_queries, memory_keys[group_id, head_id], memory_values[group_id, head_id],
                             probe_blocks[group_id, head_id], probe_counts[group_id, head_id])

        maxima, totals, weighted = lax.map(per_group, jnp.arange(GROUPS, dtype=jnp.int32))
        highest = jnp.max(maxima, axis=0)
        factor = jnp.exp(maxima - highest[None, :])
        total = jnp.sum(totals * factor, axis=0)
        summed = jnp.sum(weighted * factor[:, :, None], axis=0)
        return (summed / total[:, None]).astype(jnp.bfloat16)

    reads = lax.map(per_head, jnp.arange(HEADS, dtype=jnp.int32))
    memory_read = jnp.transpose(reads, (1, 0, 2)).reshape(TOKENS, D)
    opening = jnp.repeat(jax.nn.sigmoid(gate_logits), DH)
    mixed = opening * memory_read.astype(jnp.float32) + (1.0 - opening) * local_read.astype(jnp.float32)
    return mixed.astype(jnp.bfloat16)
```

```python
import functools
import math

import jax
import jax.numpy as jnp
from jax import lax
from jax.experimental import pallas as pl
from jax.experimental.pallas import tpu as pltpu
from jax.sharding import PartitionSpec as P

DH = 128
BLOCK = 128
PMAX = 16
GROUPS = 16
HEADS = 32
KEYS = PMAX * BLOCK
SCALE = DH ** -0.5 * math.log2(math.e)
MESH = pl.DeviceIdType.MESH

PHASES = 2
ROUNDS = 4
PART = 128 // PHASES
CHUNK = 2 * PART
TILE = 256
VROWS = 144
MSG = 144
NEUTRAL = -1e30


def add(a, b):
    return b if a is None else a + b


def load_message(ref):
    o = ref[0:DH, :].astype(jnp.float32)
    stats = ref[DH:MSG, :].astype(jnp.float32)
    m = stats[0:1] + stats[1:2] + stats[2:3]
    l = stats[3:4] + stats[4:5] + stats[5:6]
    return o, m, l


def pieces(x):
    hi = x.astype(jnp.bfloat16).astype(jnp.float32)
    rest = x - hi
    mid = rest.astype(jnp.bfloat16).astype(jnp.float32)
    return hi, mid, rest - mid


def store_message(ref, o, m, l):
    ref[0:DH, :] = o.astype(ref.dtype)
    row = lax.broadcasted_iota(jnp.int32, (MSG - DH, CHUNK), 0)
    stats = jnp.zeros((MSG - DH, CHUNK), jnp.float32)
    for i, piece in enumerate(pieces(m) + pieces(l)):
        stats = jnp.where(row == i, piece, stats)
    ref[DH:MSG, :] = stats.astype(ref.dtype)


def merge(parts):
    top = parts[0][1]
    for _, m, _ in parts[1:]:
        top = jnp.maximum(top, m)
    o = l = None
    for po, pm, pn in parts:
        factor = jnp.exp2((pm - top) * SCALE)
        o = add(o, po * factor)
        l = add(l, pn * factor)
    return o, top, l


def kernel(
    blocks_ref, count_ref, q_ref, k_ref, v_ref, read_ref,
    qa, kp, vt, scores, own_o, own_s, out_buf, in_buf, result,
    q_send, q_recv, m_send, m_recv, r_send, r_recv,
):
    g = lax.axis_index("index")
    h = lax.axis_index("head")

    def plane(step):
        return lax.rem(g + step + 2 * GROUPS, GROUPS)

    barrier = pltpu.get_barrier_semaphore()

    def greet(i, _):
        pl.semaphore_signal(barrier, inc=1, device_id=(g, lax.rem(h + i, HEADS)), device_id_type=MESH)
        return 0

    lax.fori_loop(1, HEADS, greet, 0)
    for step in (-2, -1, 1, 2):
        pl.semaphore_signal(barrier, inc=1, device_id=(plane(step), h), device_id_type=MESH)
    pl.semaphore_wait(barrier, HEADS - 1 + 4)

    for p in range(PHASES):

        def send_rows(i, _):
            to = lax.rem(h + i, HEADS)
            pltpu.make_async_remote_copy(
                src_ref=q_ref.at[pl.ds(p * PART, PART), pl.ds(pl.multiple_of(to * DH, DH), DH)],
                dst_ref=qa.at[p, pl.ds(pl.multiple_of(h * PART, PART), PART), :],
                send_sem=q_send.at[p],
                recv_sem=q_recv.at[p],
                device_id=(g, to),
                device_id_type=MESH,
            ).start()
            return 0

        lax.fori_loop(1, HEADS, send_rows, 0)
        qa[p, pl.ds(pl.multiple_of(h * PART, PART), PART), :] = q_ref[
            pl.ds(p * PART, PART), pl.ds(pl.multiple_of(h * DH, DH), DH)
        ]

    def wait_rows(p):
        part = qa.at[p, pl.ds(0, (HEADS - 1) * PART), :]
        pltpu.make_async_copy(part, part, q_recv.at[p]).wait()

    count = count_ref[0, 0]
    first = blocks_ref[0, 0, 0]
    row = lax.broadcasted_iota(jnp.int32, (VROWS - DH, BLOCK), 0)
    for j in range(PMAX):
        live = lax.div(count + (PMAX - 1 - j), PMAX)
        block = first + live * (blocks_ref[0, 0, j] - first)
        span = pl.ds(j * BLOCK, BLOCK)
        kp[span, :] = k_ref[block]
        gain = live.astype(jnp.float32)
        values = v_ref[block].astype(jnp.float32) * gain
        vt[0:DH, span] = values.T.astype(jnp.bfloat16)
        vt[DH:VROWS, span] = jnp.where(row == 0, gain, 0.0).astype(jnp.bfloat16)

    def blank(slot):
        zero = jnp.zeros((DH, CHUNK), jnp.float32)
        line = jnp.zeros((1, CHUNK), jnp.float32)
        store_message(slot, zero, line + NEUTRAL, line)

    for p in range(PHASES):
        blank(in_buf.at[0, p, 0])
        blank(in_buf.at[1, p, 0])
        blank(in_buf.at[2, p, 0])
        blank(in_buf.at[2, p, 1])
        blank(in_buf.at[3, p, 0])

    hop = (2, 1, -2, -1)

    def message(kind, p, r):
        return pltpu.make_async_remote_copy(
            src_ref=out_buf.at[kind, p, r],
            dst_ref=in_buf.at[kind, p, r + 1],
            send_sem=m_send.at[kind, p, r],
            recv_sem=m_recv.at[kind, p, r],
            device_id=(plane(hop[kind]), h),
            device_id_type=MESH,
        )

    def arrived(kind, p, r):
        message(kind, p, r).wait_recv()

    def schedule(i):
        p = 1 - lax.rem(i, 2) + lax.div(i, 7) - lax.div(7 - i, 7)
        r = (1 - p) * lax.div(i + 1, 2) + p * (lax.div(i, 2) - 1 + lax.div(i, 7))
        return p, r

    def rows_of(p, step):
        return qa[p, pl.ds(pl.multiple_of(plane(step) * CHUNK, CHUNK), CHUNK), :]

    def right_rows(p, r):
        return jnp.concatenate([rows_of(p, 8 - 2 * r), rows_of(p, 7 - 2 * r)], axis=0)

    def left_rows(p, r):
        even = (8 - 2 * r) * lax.div(r + 3, 4)
        return jnp.concatenate([rows_of(p, -even), rows_of(p, 2 * r - 7)], axis=0)

    def score_tile(q, slot, k):
        s = lax.dot_general(
            kp[k : k + TILE, :], q, (((1,), (1,)), ((), ())), preferred_element_type=jnp.float32
        )
        scores[slot, k : k + TILE, :] = s
        return jnp.max(s.reshape(TILE // 8, 8, 2 * CHUNK), axis=0)

    def value_tile(slot, m, k):
        w = jnp.exp2((scores[slot, k : k + TILE, :] - m) * SCALE).astype(jnp.bfloat16)
        return jnp.dot(vt[:, k : k + TILE], w, preferred_element_type=jnp.float32)

    def unit(q_next, m, slot):
        top = acc = None
        for k in range(0, KEYS, TILE):
            t = score_tile(q_next, 1 - slot, k)
            top = t if top is None else jnp.maximum(top, t)
            acc = add(acc, value_tile(slot, m, k))
        return acc, jnp.max(top, axis=0, keepdims=True)

    def halves(acc, m):
        even = (acc[0:DH, 0:CHUNK], m[:, 0:CHUNK], acc[DH : DH + 1, 0:CHUNK])
        odd = (acc[0:DH, CHUNK:], m[:, CHUNK:], acc[DH : DH + 1, CHUNK:])
        return even, odd

    def received(kind, p, slot):
        return load_message(in_buf.at[kind, p, slot])

    wait_rows(0)
    q = right_rows(0, 0)
    top = None
    for k in range(0, KEYS, TILE):
        t = score_tile(q, 0, k)
        top = t if top is None else jnp.maximum(top, t)
    top = jnp.max(top, axis=0, keepdims=True)

    def body(i, m_right):
        p, r = schedule(i)
        acc, m_left = unit(left_rows(p, r), m_right, 0)
        even, odd = halves(acc, m_right)
        store_message(out_buf.at[1, p, r], *odd)
        message(1, p, r).start()

        @pl.when(r > 0)
        def _():
            arrived(0, p, r - 1)
            arrived(1, p, r - 1)

        store_message(out_buf.at[0, p, r], *merge([received(0, p, r), received(1, p, r), even]))
        message(0, p, r).start()

        @pl.when(i == 1)
        def _():
            wait_rows(1)

        pn, rn = schedule(i + 1 - lax.div(i + 1, 8))
        acc, m_next = unit(right_rows(pn, rn), m_left, 1)
        even, odd = halves(acc, m_left)
        store_message(out_buf.at[3, p, r], *odd)
        message(3, p, r).start()

        @pl.when(r == 0)
        def _():
            own_o[p] = even[0]
            own_s[p, 0:1] = even[1]
            own_s[p, 1:2] = even[2]

        @pl.when(r > 0)
        def _():
            arrived(3, p, r - 1)

            @pl.when(r > 1)
            def _():
                arrived(2, p, r - 1)

            store_message(out_buf.at[2, p, r], *merge([received(2, p, r), received(3, p, r), even]))
            message(2, p, r).start()

        return m_next

    lax.fori_loop(0, PHASES * ROUNDS, body, top)

    for p in range(PHASES):
        for kind in range(4):
            arrived(kind, p, ROUNDS - 1)
        parts = [received(kind, p, ROUNDS) for kind in range(4)]
        parts.append((own_o[p], own_s[p, 0:1], own_s[p, 1:2]))
        o, _, l = merge(parts)
        read = (o / l).T.astype(jnp.bfloat16).astype(jnp.float32)
        result[p] = read

        def give(b, _):
            to = lax.div(b, 8) * 16 + 8 * p + lax.rem(b, 8)

            @pl.when(to != h)
            def _():
                pltpu.make_async_remote_copy(
                    src_ref=result.at[p, pl.ds(pl.multiple_of(b * 8, 8), 8), :],
                    dst_ref=read_ref.at[:, pl.ds(pl.multiple_of(h * DH, DH), DH)],
                    send_sem=r_send,
                    recv_sem=r_recv,
                    device_id=(g, to),
                    device_id_type=MESH,
                ).start()

            @pl.when(to == h)
            def _():
                read_ref[:, pl.ds(pl.multiple_of(h * DH, DH), DH)] = result[
                    p, pl.ds(pl.multiple_of(b * 8, 8), 8), :
                ]

            return 0

        lax.fori_loop(0, 16, give, 0)

    for p in range(PHASES):
        part = qa.at[p, pl.ds(0, (HEADS - 1) * PART), :]
        pltpu.make_async_copy(part, part, q_send.at[p]).wait()
        for kind in range(4):
            for r in range(ROUNDS):
                if kind == 2 and r == 0:
                    continue
                message(kind, p, r).wait_send()
    span = read_ref.at[:, pl.ds(0, (HEADS - 1) * DH)]
    pltpu.make_async_copy(span, span, r_send).wait()
    pltpu.make_async_copy(span, span, r_recv).wait()


def memory_reads(queries, memory_keys, memory_values, probe_blocks, probe_counts):
    vmem = pl.BlockSpec(memory_space=pltpu.VMEM)
    smem = pl.BlockSpec(memory_space=pltpu.SMEM)
    return pl.pallas_call(
        kernel,
        out_shape=jax.ShapeDtypeStruct((8, HEADS * DH), jnp.float32),
        in_specs=[smem, smem, vmem, vmem, vmem],
        out_specs=vmem,
        scratch_shapes=[
            pltpu.VMEM((PHASES, HEADS * PART, DH), jnp.bfloat16),
            pltpu.VMEM((KEYS, DH), jnp.bfloat16),
            pltpu.VMEM((VROWS, KEYS), jnp.bfloat16),
            pltpu.VMEM((2, KEYS, 2 * CHUNK), jnp.float32),
            pltpu.VMEM((PHASES, DH, CHUNK), jnp.float32),
            pltpu.VMEM((PHASES, 8, CHUNK), jnp.float32),
            pltpu.VMEM((4, PHASES, ROUNDS, MSG, CHUNK), jnp.bfloat16),
            pltpu.VMEM((4, PHASES, ROUNDS + 1, MSG, CHUNK), jnp.bfloat16),
            pltpu.VMEM((PHASES, CHUNK, DH), jnp.float32),
            pltpu.SemaphoreType.DMA((PHASES,)),
            pltpu.SemaphoreType.DMA((PHASES,)),
            pltpu.SemaphoreType.DMA((4, PHASES, ROUNDS)),
            pltpu.SemaphoreType.DMA((4, PHASES, ROUNDS)),
            pltpu.SemaphoreType.DMA,
            pltpu.SemaphoreType.DMA,
        ],
        compiler_params=pltpu.CompilerParams(
            collective_id=0, has_side_effects=True, vmem_limit_bytes=48 << 20
        ),
        name="memory_reads",
    )(
        probe_blocks,
        probe_counts,
        queries,
        memory_keys.reshape(-1, BLOCK, DH),
        memory_values.reshape(-1, BLOCK, DH),
    )


def local(queries, local_read, gate_logits, memory_keys, memory_values, probe_blocks, probe_counts):
    reads = memory_reads(queries, memory_keys, memory_values, probe_blocks, probe_counts)
    opening = jnp.repeat(jax.nn.sigmoid(gate_logits), DH)
    mixed = opening * reads + (1.0 - opening) * local_read.astype(jnp.float32)
    return mixed.astype(jnp.bfloat16)


def solution(mesh):
    return jax.shard_map(
        local,
        mesh=mesh,
        in_specs=(
            P("head", None),
            P(("index", "head"), None),
            P(),
            P("index", "head", None, None),
            P("index", "head", None, None),
            P("index", "head", None),
            P("index", "head"),
        ),
        out_specs=P(("index", "head"), None),
        check_vma=False,
    )
```

```python
import functools
import math

import jax
import jax.numpy as jnp
from jax import lax
from jax.experimental import pallas as pl
from jax.experimental.pallas import tpu as pltpu
from jax.sharding import PartitionSpec as P

DH = 128
BLOCK = 128
PMAX = 16
GROUPS = 16
HEADS = 32
KEYS = PMAX * BLOCK
SCALE = DH ** -0.5 * math.log2(math.e)
MESH = pl.DeviceIdType.MESH

PHASES = 2
ROUNDS = 4
PART = 128 // PHASES
CHUNK = 2 * PART
TILE = 256
VROWS = 144
MSG = 144


def add(a, b):
    return b if a is None else a + b


def load_message(ref):
    o = ref[0:DH, :].astype(jnp.float32)
    stats = ref[DH:MSG, :].astype(jnp.float32)
    m = stats[0:1] + stats[1:2] + stats[2:3]
    l = stats[3:4] + stats[4:5] + stats[5:6]
    return o, m, l


def pieces(x):
    hi = x.astype(jnp.bfloat16).astype(jnp.float32)
    rest = x - hi
    mid = rest.astype(jnp.bfloat16).astype(jnp.float32)
    return hi, mid, rest - mid


def store_message(ref, o, m, l):
    ref[0:DH, :] = o.astype(ref.dtype)
    row = lax.broadcasted_iota(jnp.int32, (MSG - DH, CHUNK), 0)
    stats = jnp.zeros((MSG - DH, CHUNK), jnp.float32)
    for i, piece in enumerate(pieces(m) + pieces(l)):
        stats = jnp.where(row == i, piece, stats)
    ref[DH:MSG, :] = stats.astype(ref.dtype)


def merge(parts):
    top = parts[0][1]
    for _, m, _ in parts[1:]:
        top = jnp.maximum(top, m)
    o = l = None
    for po, pm, pn in parts:
        factor = jnp.exp2((pm - top) * SCALE)
        o = add(o, po * factor)
        l = add(l, pn * factor)
    return o, top, l


def kernel(
    blocks_hbm, count_hbm, gate_hbm, q_ref, k_hbm, v_hbm, near_hbm, mixed_ref,
    blocks_ref, count_ref, gate_ref, k_ref, v_ref, near_ref, opening, read_ref,
    qa, kp, vt, scores, part_o, part_s, out_buf, in_buf, result,
    load_sem, q_send, q_recv, m_send, m_recv, r_send, r_recv,
):
    g = lax.axis_index("index")
    h = lax.axis_index("head")

    def plane(step):
        return lax.rem(g + step + 2 * GROUPS, GROUPS)

    own_rows = [
        pltpu.make_async_copy(
            q_ref.at[pl.ds(p * PART, PART), pl.ds(pl.multiple_of(h * DH, DH), DH)],
            qa.at[p, pl.ds(pl.multiple_of(h * PART, PART), PART), :],
            load_sem.at[p],
        )
        for p in range(PHASES)
    ]
    loads = [
        pltpu.make_async_copy(src, dst, load_sem.at[PHASES + i])
        for i, (src, dst) in enumerate(
            (
                (blocks_hbm, blocks_ref),
                (count_hbm, count_ref),
                (gate_hbm, gate_ref),
                (k_hbm, k_ref),
                (v_hbm, v_ref),
                (near_hbm, near_ref),
            )
        )
    ]
    for copy in loads + own_rows:
        copy.start()

    barrier = pltpu.get_barrier_semaphore()

    def greet(i, _):
        pl.semaphore_signal(barrier, inc=1, device_id=(g, lax.rem(h + i, HEADS)), device_id_type=MESH)
        return 0

    lax.fori_loop(1, HEADS, greet, 0)
    for step in (-2, -1, 1, 2):
        pl.semaphore_signal(barrier, inc=1, device_id=(plane(step), h), device_id_type=MESH)
    pl.semaphore_wait(barrier, HEADS - 1 + 4)

    for p in range(PHASES):

        def send_rows(i, _):
            to = lax.rem(h + i, HEADS)
            pltpu.make_async_remote_copy(
                src_ref=q_ref.at[pl.ds(p * PART, PART), pl.ds(pl.multiple_of(to * DH, DH), DH)],
                dst_ref=qa.at[p, pl.ds(pl.multiple_of(h * PART, PART), PART), :],
                send_sem=q_send.at[p],
                recv_sem=q_recv.at[p],
                device_id=(g, to),
                device_id_type=MESH,
            ).start()
            return 0

        lax.fori_loop(1, HEADS, send_rows, 0)

    def wait_rows(p):
        own_rows[p].wait()
        part = qa.at[p, pl.ds(0, (HEADS - 1) * PART), :]
        pltpu.make_async_copy(part, part, q_recv.at[p]).wait()

    for copy in loads:
        copy.wait()
    count = count_ref[0, 0]
    first = blocks_ref[0, 0, 0]
    row = lax.broadcasted_iota(jnp.int32, (VROWS - DH, BLOCK), 0)
    for j in range(PMAX):
        live = lax.div(count + (PMAX - 1 - j), PMAX)
        block = first + live * (blocks_ref[0, 0, j] - first)
        span = pl.ds(j * BLOCK, BLOCK)
        kp[span, :] = k_ref[block]
        gain = live.astype(jnp.float32)
        values = v_ref[block].astype(jnp.float32) * gain
        vt[0:DH, span] = values.T.astype(jnp.bfloat16)
        vt[DH:VROWS, span] = jnp.where(row == 0, gain, 0.0).astype(jnp.bfloat16)

    for j in range(HEADS):
        logit = jnp.full((8, DH), gate_ref[j], jnp.float32)
        opening[:, j * DH : (j + 1) * DH] = 1.0 / (1.0 + jnp.exp(-logit))

    hop = (2, 1, -2, -1)

    def message(kind, p, r):
        return pltpu.make_async_remote_copy(
            src_ref=out_buf.at[kind, p, r],
            dst_ref=in_buf.at[kind, p, r + 1],
            send_sem=m_send.at[kind, p, r],
            recv_sem=m_recv.at[kind, p, r],
            device_id=(plane(hop[kind]), h),
            device_id_type=MESH,
        )

    def arrived(kind, p, r):
        message(kind, p, r).wait_recv()

    def from_step(i, a):
        return lax.div(i + (8 - a), 8)

    def schedule(i):
        p = from_step(i, 3) - from_step(i, 5) + from_step(i, 6)
        r = i - 3 * from_step(i, 3) + from_step(i, 5) - 2 * from_step(i, 6)
        return p, r

    def rows_of(p, step):
        return qa[p, pl.ds(pl.multiple_of(plane(step) * CHUNK, CHUNK), CHUNK), :]

    def right_rows(p, r):
        return jnp.concatenate([rows_of(p, 8 - 2 * r), rows_of(p, 7 - 2 * r)], axis=0)

    def left_rows(p, r):
        even = (8 - 2 * r) * lax.div(r + 3, 4)
        return jnp.concatenate([rows_of(p, -even), rows_of(p, 2 * r - 7)], axis=0)

    def score_tile(q, slot, k):
        s = lax.dot_general(
            kp[k : k + TILE, :], q, (((1,), (1,)), ((), ())), preferred_element_type=jnp.float32
        )
        scores[slot, k : k + TILE, :] = s
        return jnp.max(s.reshape(TILE // 8, 8, 2 * CHUNK), axis=0)

    def value_tile(slot, m, k):
        w = jnp.exp2((scores[slot, k : k + TILE, :] - m) * SCALE).astype(jnp.bfloat16)
        return jnp.dot(vt[:, k : k + TILE], w, preferred_element_type=jnp.float32)

    def unit(q_next, m, slot):
        top = acc = None
        for k in range(0, KEYS, TILE):
            t = score_tile(q_next, 1 - slot, k)
            top = t if top is None else jnp.maximum(top, t)
            acc = add(acc, value_tile(slot, m, k))
        return acc, jnp.max(top, axis=0, keepdims=True)

    def halves(acc, m):
        even = (acc[0:DH, 0:CHUNK], m[:, 0:CHUNK], acc[DH : DH + 1, 0:CHUNK])
        odd = (acc[0:DH, CHUNK:], m[:, CHUNK:], acc[DH : DH + 1, CHUNK:])
        return even, odd

    def received(kind, p, slot):
        return load_message(in_buf.at[kind, p, slot])

    wait_rows(0)
    q = right_rows(0, 0)
    top = None
    for k in range(0, KEYS, TILE):
        t = score_tile(q, 0, k)
        top = t if top is None else jnp.maximum(top, t)
    top = jnp.max(top, axis=0, keepdims=True)

    def keep(side, p, r, part):
        part_o[side, p, r] = part[0]
        part_s[side, p, r, 0:1] = part[1]
        part_s[side, p, r, 1:2] = part[2]

    def kept(side, p, r):
        return part_o[side, p, r], part_s[side, p, r, 0:1], part_s[side, p, r, 1:2]

    def pass_on(p, r):
        for side in range(2):
            parts = [kept(side, p, r)]
            for kind in (2 * side, 2 * side + 1):
                if kind == 2 and r == 1:
                    continue
                arrived(kind, p, r - 1)
                parts.append(received(kind, p, r))
            store_message(out_buf.at[2 * side, p, r], *merge(parts))
            message(2 * side, p, r).start()

    def body(i, m_right):
        p, r = schedule(i)
        acc, m_left = unit(left_rows(p, r), m_right, 0)
        even, odd = halves(acc, m_right)
        store_message(out_buf.at[1, p, r], *odd)
        message(1, p, r).start()

        @pl.when(r == 0)
        def _():
            store_message(out_buf.at[0, p, r], *even)
            message(0, p, r).start()

        @pl.when(r > 0)
        def _():
            keep(0, p, r, even)

        @pl.when(i == 2)
        def _():
            wait_rows(1)

        pn, rn = schedule(i + 1 - lax.div(i + 1, 8))
        acc, m_next = unit(right_rows(pn, rn), m_left, 1)
        even, odd = halves(acc, m_left)
        store_message(out_buf.at[3, p, r], *odd)
        message(3, p, r).start()
        keep(1, p, r, even)

        @pl.when(i == 3)
        def _():
            pass_on(0, 1)

        @pl.when(i == 5)
        def _():
            pass_on(1, 1)
            pass_on(0, 2)

        return m_next

    lax.fori_loop(0, PHASES * ROUNDS, body, top)
    pass_on(1, 2)
    pass_on(0, 3)
    pass_on(1, 3)

    for p in range(PHASES):
        for kind in range(4):
            arrived(kind, p, ROUNDS - 1)
        parts = [received(kind, p, ROUNDS) for kind in range(4)]
        parts.append(kept(1, p, 0))
        o, _, l = merge(parts)
        read = (o / l).T.astype(jnp.bfloat16).astype(jnp.float32)
        result[p] = read

        def give(b, _):
            to = lax.div(b, 8) * 16 + 8 * p + lax.rem(b, 8)

            @pl.when(to != h)
            def _():
                pltpu.make_async_remote_copy(
                    src_ref=result.at[p, pl.ds(pl.multiple_of(b * 8, 8), 8), :],
                    dst_ref=read_ref.at[:, pl.ds(pl.multiple_of(h * DH, DH), DH)],
                    send_sem=r_send,
                    recv_sem=r_recv,
                    device_id=(g, to),
                    device_id_type=MESH,
                ).start()

            @pl.when(to == h)
            def _():
                read_ref[:, pl.ds(pl.multiple_of(h * DH, DH), DH)] = result[
                    p, pl.ds(pl.multiple_of(b * 8, 8), 8), :
                ]

            return 0

        lax.fori_loop(0, 16, give, 0)

    for p in range(PHASES):
        part = qa.at[p, pl.ds(0, (HEADS - 1) * PART), :]
        pltpu.make_async_copy(part, part, q_send.at[p]).wait()
        for kind in range(4):
            for r in range(ROUNDS):
                if kind == 2 and r == 0:
                    continue
                message(kind, p, r).wait_send()
    span = read_ref.at[:, pl.ds(0, (HEADS - 1) * DH)]
    pltpu.make_async_copy(span, span, r_send).wait()
    pltpu.make_async_copy(span, span, r_recv).wait()
    gate = opening[...]
    near = near_ref[...].astype(jnp.float32)
    mixed_ref[...] = (gate * read_ref[...] + (1.0 - gate) * near).astype(jnp.bfloat16)


def local(queries, local_read, gate_logits, memory_keys, memory_values, probe_blocks, probe_counts):
    vmem = pl.BlockSpec(memory_space=pltpu.VMEM)
    hbm = pl.BlockSpec(memory_space=pl.ANY)
    return pl.pallas_call(
        kernel,
        out_shape=jax.ShapeDtypeStruct((8, HEADS * DH), jnp.bfloat16),
        in_specs=[hbm] * 7,
        out_specs=vmem,
        scratch_shapes=[
            pltpu.SMEM((1, 1, PMAX), jnp.int32),
            pltpu.SMEM((1, 1), jnp.int32),
            pltpu.SMEM((HEADS,), jnp.float32),
            pltpu.VMEM((32, BLOCK, DH), jnp.bfloat16),
            pltpu.VMEM((32, BLOCK, DH), jnp.bfloat16),
            pltpu.VMEM((8, HEADS * DH), jnp.bfloat16),
            pltpu.VMEM((8, HEADS * DH), jnp.float32),
            pltpu.VMEM((8, HEADS * DH), jnp.float32),
            pltpu.VMEM((PHASES, HEADS * PART, DH), jnp.bfloat16),
            pltpu.VMEM((KEYS, DH), jnp.bfloat16),
            pltpu.VMEM((VROWS, KEYS), jnp.bfloat16),
            pltpu.VMEM((2, KEYS, 2 * CHUNK), jnp.float32),
            pltpu.VMEM((2, PHASES, ROUNDS, DH, CHUNK), jnp.float32),
            pltpu.VMEM((2, PHASES, ROUNDS, 8, CHUNK), jnp.float32),
            pltpu.VMEM((4, PHASES, ROUNDS, MSG, CHUNK), jnp.bfloat16),
            pltpu.VMEM((4, PHASES, ROUNDS + 1, MSG, CHUNK), jnp.bfloat16),
            pltpu.VMEM((PHASES, CHUNK, DH), jnp.float32),
            pltpu.SemaphoreType.DMA((PHASES + 6,)),
            pltpu.SemaphoreType.DMA((PHASES,)),
            pltpu.SemaphoreType.DMA((PHASES,)),
            pltpu.SemaphoreType.DMA((4, PHASES, ROUNDS)),
            pltpu.SemaphoreType.DMA((4, PHASES, ROUNDS)),
            pltpu.SemaphoreType.DMA,
            pltpu.SemaphoreType.DMA,
        ],
        compiler_params=pltpu.CompilerParams(
            collective_id=0, has_side_effects=True, vmem_limit_bytes=63 << 20
        ),
        name="memory_reads",
    )(
        probe_blocks,
        probe_counts,
        gate_logits,
        queries,
        memory_keys.reshape(-1, BLOCK, DH),
        memory_values.reshape(-1, BLOCK, DH),
        local_read,
    )


def solution(mesh):
    return jax.shard_map(
        local,
        mesh=mesh,
        in_specs=(
            P("head", None),
            P(("index", "head"), None),
            P(),
            P("index", "head", None, None),
            P("index", "head", None, None),
            P("index", "head", None),
            P("index", "head"),
        ),
        out_specs=P(("index", "head"), None),
        check_vma=False,
    )
```

```python
import functools
import math

import jax
import jax.numpy as jnp
from jax import lax
from jax.experimental import pallas as pl
from jax.experimental.pallas import tpu as pltpu
from jax.sharding import PartitionSpec as P

DH = 128
BLOCK = 128
PMAX = 16
GROUPS = 16
HEADS = 32
KEYS = PMAX * BLOCK
SCALE = DH ** -0.5 * math.log2(math.e)
MESH = pl.DeviceIdType.MESH

PHASES = 2
ROUNDS = 4
PART = 128 // PHASES
CHUNK = 2 * PART
TILE = 256
VROWS = 144


def add(a, b):
    return b if a is None else a + b


def merge(parts):
    top = parts[0][1]
    for _, m, _ in parts[1:]:
        top = jnp.maximum(top, m)
    o = l = None
    for po, pm, pn in parts:
        factor = jnp.exp2((pm - top) * SCALE)
        o = add(o, po * factor)
        l = add(l, pn * factor)
    return o, top, l


def kernel(
    blocks_hbm, count_hbm, gate_hbm, q_ref, k_hbm, v_hbm, near_hbm, mixed_ref,
    blocks_ref, count_ref, gate_ref, k_ref, v_ref, near_ref, opening, read_ref,
    qa, kp, vt, scores, part_o, part_s, out_o, out_s, in_o, in_s, result,
    load_sem, q_send, q_recv, m_send, m_recv, s_send, s_recv, r_send, r_recv,
):
    g = lax.axis_index("index")
    h = lax.axis_index("head")

    def plane(step):
        return lax.rem(g + step + 2 * GROUPS, GROUPS)

    own_rows = [
        pltpu.make_async_copy(
            q_ref.at[pl.ds(p * PART, PART), pl.ds(pl.multiple_of(h * DH, DH), DH)],
            qa.at[p, pl.ds(pl.multiple_of(h * PART, PART), PART), :],
            load_sem.at[p],
        )
        for p in range(PHASES)
    ]
    loads = [
        pltpu.make_async_copy(src, dst, load_sem.at[PHASES + i])
        for i, (src, dst) in enumerate(
            (
                (blocks_hbm, blocks_ref),
                (count_hbm, count_ref),
                (gate_hbm, gate_ref),
                (k_hbm, k_ref),
                (v_hbm, v_ref),
                (near_hbm, near_ref),
            )
        )
    ]
    for copy in loads + own_rows:
        copy.start()

    barrier = pltpu.get_barrier_semaphore()

    def greet(i, _):
        pl.semaphore_signal(barrier, inc=1, device_id=(g, lax.rem(h + i, HEADS)), device_id_type=MESH)
        return 0

    lax.fori_loop(1, HEADS, greet, 0)
    for step in (-2, -1, 1, 2):
        pl.semaphore_signal(barrier, inc=1, device_id=(plane(step), h), device_id_type=MESH)
    pl.semaphore_wait(barrier, HEADS - 1 + 4)

    for p in range(PHASES):

        def send_rows(i, _):
            s, t = lax.rem(i, 4), lax.div(i, 8)
            dx = 1 + 2 * s - 3 * lax.div(s, 2)
            dy = 2 - t + 3 * lax.div(t, 2) - 2 * lax.div(t, 3)
            x, y = lax.rem(lax.div(h, 8) + dx, 4), lax.rem(lax.rem(lax.div(h, 2), 4) + dy, 4)
            to = 8 * x + 2 * y + lax.rem(lax.rem(h, 2) + lax.rem(lax.div(i, 4), 2), 2)

            pltpu.make_async_remote_copy(
                src_ref=q_ref.at[pl.ds(p * PART, PART), pl.ds(pl.multiple_of(to * DH, DH), DH)],
                dst_ref=qa.at[p, pl.ds(pl.multiple_of(h * PART, PART), PART), :],
                send_sem=q_send.at[p],
                recv_sem=q_recv.at[p],
                device_id=(g, to),
                device_id_type=MESH,
            ).start()
            return 0

        lax.fori_loop(0, 27, send_rows, 0)
        lax.fori_loop(28, HEADS, send_rows, 0)

    def wait_rows(p):
        own_rows[p].wait()
        part = qa.at[p, pl.ds(0, (HEADS - 1) * PART), :]
        pltpu.make_async_copy(part, part, q_recv.at[p]).wait()

    for copy in loads:
        copy.wait()
    count = count_ref[0, 0]
    first = blocks_ref[0, 0, 0]
    row = lax.broadcasted_iota(jnp.int32, (VROWS - DH, BLOCK), 0)
    for j in range(PMAX):
        live = lax.div(count + (PMAX - 1 - j), PMAX)
        block = first + live * (blocks_ref[0, 0, j] - first)
        span = pl.ds(j * BLOCK, BLOCK)
        kp[span, :] = k_ref[block]
        gain = live.astype(jnp.float32)
        values = v_ref[block].astype(jnp.float32) * gain
        vt[0:DH, span] = values.T.astype(jnp.bfloat16)
        vt[DH:VROWS, span] = jnp.where(row == 0, gain, 0.0).astype(jnp.bfloat16)

    for j in range(HEADS):
        logit = jnp.full((8, DH), gate_ref[j], jnp.float32)
        opening[:, j * DH : (j + 1) * DH] = 1.0 / (1.0 + jnp.exp(-logit))

    hop = (2, 1, -2, -1)

    def message(kind, p, r, step=None):
        to = plane(hop[kind] if step is None else step)
        return [
            pltpu.make_async_remote_copy(
                src_ref=src, dst_ref=dst, send_sem=send, recv_sem=recv, device_id=(to, h), device_id_type=MESH
            )
            for src, dst, send, recv in (
                (
                    out_s.at[kind, p, r, pl.ds(0, 2)],
                    in_s.at[kind, p, r, pl.ds(0, 2)],
                    s_send.at[kind, p, r],
                    s_recv.at[kind, p, r],
                ),
                (out_o.at[kind, p, r], in_o.at[kind, p, r], m_send.at[kind, p, r], m_recv.at[kind, p, r]),
            )
        ]

    def send(kind, p, r, part, step=None):
        out_o[kind, p, r] = part[0].astype(jnp.bfloat16)
        out_s[kind, p, r, 0:1] = part[1]
        out_s[kind, p, r, 1:2] = part[2]
        for copy in message(kind, p, r, step):
            copy.start()

    def receive(kind, p, r):
        for copy in message(kind, p, r):
            copy.wait_recv()
        return in_o[kind, p, r].astype(jnp.float32), in_s[kind, p, r, 0:1], in_s[kind, p, r, 1:2]

    def from_step(i, a):
        return lax.div(i + (8 - a), 8)

    def schedule(i):
        p = from_step(i, 3) - from_step(i, 5) + from_step(i, 6)
        r = i - 3 * from_step(i, 3) + from_step(i, 5) - 2 * from_step(i, 6)
        return p, r

    def rows_of(p, step):
        return qa[p, pl.ds(pl.multiple_of(plane(step) * CHUNK, CHUNK), CHUNK), :]

    def right_rows(p, r):
        return jnp.concatenate([rows_of(p, 8 - 2 * r), rows_of(p, 7 - 2 * r)], axis=0)

    def left_rows(p, r):
        even = (8 - 2 * r) * lax.div(r + 3, 4)
        return jnp.concatenate([rows_of(p, -even), rows_of(p, 2 * r - 7)], axis=0)

    def score_tile(q, slot, k):
        s = lax.dot_general(
            kp[k : k + TILE, :], q, (((1,), (1,)), ((), ())), preferred_element_type=jnp.float32
        )
        scores[slot, k : k + TILE, :] = s
        return jnp.max(s.reshape(TILE // 8, 8, 2 * CHUNK), axis=0)

    def value_tile(slot, m, k):
        w = jnp.exp2((scores[slot, k : k + TILE, :] - m) * SCALE).astype(jnp.bfloat16)
        return jnp.dot(vt[:, k : k + TILE], w, preferred_element_type=jnp.float32)

    def unit(q_next, m, slot):
        top = acc = None
        for k in range(0, KEYS, TILE):
            t = score_tile(q_next, 1 - slot, k)
            top = t if top is None else jnp.maximum(top, t)
            acc = add(acc, value_tile(slot, m, k))
        return acc, jnp.max(top, axis=0, keepdims=True)

    def halves(acc, m):
        even = (acc[0:DH, 0:CHUNK], m[:, 0:CHUNK], acc[DH : DH + 1, 0:CHUNK])
        odd = (acc[0:DH, CHUNK:], m[:, CHUNK:], acc[DH : DH + 1, CHUNK:])
        return even, odd

    wait_rows(0)
    q = right_rows(0, 0)
    top = None
    for k in range(0, KEYS, TILE):
        t = score_tile(q, 0, k)
        top = t if top is None else jnp.maximum(top, t)
    top = jnp.max(top, axis=0, keepdims=True)

    def keep(side, p, r, part):
        part_o[side, p, r] = part[0]
        part_s[side, p, r, 0:1] = part[1]
        part_s[side, p, r, 1:2] = part[2]

    def kept(side, p, r):
        return part_o[side, p, r], part_s[side, p, r, 0:1], part_s[side, p, r, 1:2]

    def pass_on(p, r):
        for side in range(2):
            parts = [kept(side, p, r)]
            if r > 1 or (side == 0 and p == 1):
                parts.append(receive(2 * side, p, r - 1))
            parts.append(receive(2 * side + 1, p, r - 1))
            send(2 * side, p, r, merge(parts))

    def body(i, m_right):
        p, r = schedule(i)
        acc, m_left = unit(left_rows(p, r), m_right, 0)
        even, odd = halves(acc, m_right)

        @pl.when(r == 0)
        def _():
            send(0, p, r, even, 1 + p)

        @pl.when(r > 0)
        def _():
            keep(0, p, r, even)

        @pl.when(i == 0)
        def _():
            keep(0, 0, 0, odd)

        @pl.when(i > 0)
        def _():
            send(1, p, r, odd)

        @pl.when(i == 2)
        def _():
            send(1, 0, 0, merge([kept(0, 0, 0), receive(0, 0, 0)]))
            wait_rows(1)

        pn, rn = schedule(i + 1 - lax.div(i + 1, 8))
        acc, m_next = unit(right_rows(pn, rn), m_left, 1)
        even, odd = halves(acc, m_left)
        send(3, p, r, odd)
        keep(1, p, r, even)

        @pl.when(i == 4)
        def _():
            pass_on(0, 1)

        @pl.when(i == 5)
        def _():
            pass_on(1, 1)

        return m_next

    lax.fori_loop(0, PHASES * ROUNDS, body, top)
    pass_on(0, 2)
    pass_on(1, 2)
    pass_on(0, 3)
    pass_on(1, 3)

    for p in range(PHASES):
        parts = [receive(kind, p, ROUNDS - 1) for kind in range(4)]
        parts.append(kept(1, p, 0))
        o, _, l = merge(parts)
        read = (o / l).T.astype(jnp.bfloat16).astype(jnp.float32)
        result[p] = read

        def give(b, _):
            to = lax.div(b, 8) * 16 + 8 * p + lax.rem(b, 8)

            @pl.when(to != h)
            def _():
                pltpu.make_async_remote_copy(
                    src_ref=result.at[p, pl.ds(pl.multiple_of(b * 8, 8), 8), :],
                    dst_ref=read_ref.at[:, pl.ds(pl.multiple_of(h * DH, DH), DH)],
                    send_sem=r_send,
                    recv_sem=r_recv,
                    device_id=(g, to),
                    device_id_type=MESH,
                ).start()

            @pl.when(to == h)
            def _():
                read_ref[:, pl.ds(pl.multiple_of(h * DH, DH), DH)] = result[
                    p, pl.ds(pl.multiple_of(b * 8, 8), 8), :
                ]

            return 0

        lax.fori_loop(0, 16, give, 0)

    for p in range(PHASES):
        part = qa.at[p, pl.ds(0, (HEADS - 1) * PART), :]
        pltpu.make_async_copy(part, part, q_send.at[p]).wait()
        for kind in range(4):
            for r in range(ROUNDS):
                if kind == 2 and r == 0:
                    continue
                for copy in message(kind, p, r):
                    copy.wait_send()
    span = read_ref.at[:, pl.ds(0, (HEADS - 1) * DH)]
    pltpu.make_async_copy(span, span, r_send).wait()
    pltpu.make_async_copy(span, span, r_recv).wait()
    gate = opening[...]
    near = near_ref[...].astype(jnp.float32)
    mixed_ref[...] = (gate * read_ref[...] + (1.0 - gate) * near).astype(jnp.bfloat16)


def local(queries, local_read, gate_logits, memory_keys, memory_values, probe_blocks, probe_counts):
    vmem = pl.BlockSpec(memory_space=pltpu.VMEM)
    hbm = pl.BlockSpec(memory_space=pl.ANY)
    return pl.pallas_call(
        kernel,
        out_shape=jax.ShapeDtypeStruct((8, HEADS * DH), jnp.bfloat16),
        in_specs=[hbm] * 7,
        out_specs=vmem,
        scratch_shapes=[
            pltpu.SMEM((1, 1, PMAX), jnp.int32),
            pltpu.SMEM((1, 1), jnp.int32),
            pltpu.SMEM((HEADS,), jnp.float32),
            pltpu.VMEM((32, BLOCK, DH), jnp.bfloat16),
            pltpu.VMEM((32, BLOCK, DH), jnp.bfloat16),
            pltpu.VMEM((8, HEADS * DH), jnp.bfloat16),
            pltpu.VMEM((8, HEADS * DH), jnp.float32),
            pltpu.VMEM((8, HEADS * DH), jnp.float32),
            pltpu.VMEM((PHASES, HEADS * PART, DH), jnp.bfloat16),
            pltpu.VMEM((KEYS, DH), jnp.bfloat16),
            pltpu.VMEM((VROWS, KEYS), jnp.bfloat16),
            pltpu.VMEM((2, KEYS, 2 * CHUNK), jnp.float32),
            pltpu.VMEM((2, PHASES, ROUNDS, DH, CHUNK), jnp.float32),
            pltpu.VMEM((2, PHASES, ROUNDS, 8, CHUNK), jnp.float32),
            pltpu.VMEM((4, PHASES, ROUNDS, DH, CHUNK), jnp.bfloat16),
            pltpu.VMEM((4, PHASES, ROUNDS, 8, CHUNK), jnp.float32),
            pltpu.VMEM((4, PHASES, ROUNDS, DH, CHUNK), jnp.bfloat16),
            pltpu.VMEM((4, PHASES, ROUNDS, 8, CHUNK), jnp.float32),
            pltpu.VMEM((PHASES, CHUNK, DH), jnp.float32),
            pltpu.SemaphoreType.DMA((PHASES + 6,)),
            pltpu.SemaphoreType.DMA((PHASES,)),
            pltpu.SemaphoreType.DMA((PHASES,)),
            pltpu.SemaphoreType.DMA((4, PHASES, ROUNDS)),
            pltpu.SemaphoreType.DMA((4, PHASES, ROUNDS)),
            pltpu.SemaphoreType.DMA((4, PHASES, ROUNDS)),
            pltpu.SemaphoreType.DMA((4, PHASES, ROUNDS)),
            pltpu.SemaphoreType.DMA,
            pltpu.SemaphoreType.DMA,
        ],
        compiler_params=pltpu.CompilerParams(
            collective_id=0, has_side_effects=True, vmem_limit_bytes=63 << 20
        ),
        name="memory_reads",
    )(
        probe_blocks,
        probe_counts,
        gate_logits,
        queries,
        memory_keys.reshape(-1, BLOCK, DH),
        memory_values.reshape(-1, BLOCK, DH),
        local_read,
    )


def solution(mesh):
    return jax.shard_map(
        local,
        mesh=mesh,
        in_specs=(
            P("head", None),
            P(("index", "head"), None),
            P(),
            P("index", "head", None, None),
            P("index", "head", None, None),
            P("index", "head", None),
            P("index", "head"),
        ),
        out_specs=P(("index", "head"), None),
        check_vma=False,
    )
```

```python
import functools
import math

import jax
import jax.numpy as jnp
from jax import lax
from jax.experimental import pallas as pl
from jax.experimental.pallas import tpu as pltpu
from jax.sharding import PartitionSpec as P

DH = 128
BLOCK = 128
PMAX = 16
GROUPS = 16
HEADS = 32
KEYS = PMAX * BLOCK
SCALE = DH ** -0.5 * math.log2(math.e)
MESH = pl.DeviceIdType.MESH

PHASES = 4
ROUNDS = 4
PART = 128 // PHASES
CHUNK = 2 * PART
FOLD = 2 * CHUNK
TILE = 256
VROWS = 144


def add(a, b):
    return b if a is None else a + b


def merge(parts):
    top = parts[0][1]
    for _, m, _ in parts[1:]:
        top = jnp.maximum(top, m)
    o = l = None
    for po, pm, pn in parts:
        factor = jnp.exp2((pm - top) * SCALE)
        o = add(o, po * factor)
        l = add(l, pn * factor)
    return o, top, l


def kernel(
    blocks_hbm, count_hbm, gate_hbm, q_ref, k_hbm, v_hbm, near_hbm, mixed_ref,
    blocks_ref, count_ref, gate_ref, k_ref, v_ref, near_ref, opening, read_ref,
    qa, kp, vt, scores, part_o, part_s, out_o, out_s, in_o, in_s, result,
    load_sem, q_send, q_recv, m_send, m_recv, s_send, s_recv, r_send, r_recv,
):
    g = lax.axis_index("index")
    h = lax.axis_index("head")

    def plane(step):
        return lax.rem(g + step + 2 * GROUPS, GROUPS)

    own_rows = [
        pltpu.make_async_copy(
            q_ref.at[pl.ds(p * PART, PART), pl.ds(pl.multiple_of(h * DH, DH), DH)],
            qa.at[p, pl.ds(pl.multiple_of(h * PART, PART), PART), :],
            load_sem.at[p],
        )
        for p in range(PHASES)
    ]
    loads = [
        pltpu.make_async_copy(src, dst, load_sem.at[PHASES + i])
        for i, (src, dst) in enumerate(
            (
                (blocks_hbm, blocks_ref),
                (count_hbm, count_ref),
                (gate_hbm, gate_ref),
                (k_hbm, k_ref),
                (v_hbm, v_ref),
                (near_hbm, near_ref),
            )
        )
    ]
    for copy in loads + own_rows:
        copy.start()

    barrier = pltpu.get_barrier_semaphore()

    def greet(i, _):
        pl.semaphore_signal(barrier, inc=1, device_id=(g, lax.rem(h + i, HEADS)), device_id_type=MESH)
        return 0

    lax.fori_loop(1, HEADS, greet, 0)
    for step in (-2, -1, 1, 2):
        pl.semaphore_signal(barrier, inc=1, device_id=(plane(step), h), device_id_type=MESH)
    pl.semaphore_wait(barrier, HEADS - 1 + 4)

    for p in range(PHASES):

        def send_rows(i, _):
            s, t = lax.rem(i, 4), lax.div(i, 8)
            dx = 1 + 2 * s - 3 * lax.div(s, 2)
            dy = 2 - t + 3 * lax.div(t, 2) - 2 * lax.div(t, 3)
            x, y = lax.rem(lax.div(h, 8) + dx, 4), lax.rem(lax.rem(lax.div(h, 2), 4) + dy, 4)
            to = 8 * x + 2 * y + lax.rem(lax.rem(h, 2) + lax.rem(lax.div(i, 4), 2), 2)

            pltpu.make_async_remote_copy(
                src_ref=q_ref.at[pl.ds(p * PART, PART), pl.ds(pl.multiple_of(to * DH, DH), DH)],
                dst_ref=qa.at[p, pl.ds(pl.multiple_of(h * PART, PART), PART), :],
                send_sem=q_send.at[p],
                recv_sem=q_recv.at[p],
                device_id=(g, to),
                device_id_type=MESH,
            ).start()
            return 0

        lax.fori_loop(0, 27, send_rows, 0)
        lax.fori_loop(28, HEADS, send_rows, 0)

    def wait_rows(p):
        own_rows[p].wait()
        part = qa.at[p, pl.ds(0, (HEADS - 1) * PART), :]
        pltpu.make_async_copy(part, part, q_recv.at[p]).wait()

    for copy in loads:
        copy.wait()
    count = count_ref[0, 0]
    first = blocks_ref[0, 0, 0]
    row = lax.broadcasted_iota(jnp.int32, (VROWS - DH, BLOCK), 0)
    for j in range(PMAX):
        live = lax.div(count + (PMAX - 1 - j), PMAX)
        block = first + live * (blocks_ref[0, 0, j] - first)
        span = pl.ds(j * BLOCK, BLOCK)
        kp[span, :] = k_ref[block]
        gain = live.astype(jnp.float32)
        values = v_ref[block].astype(jnp.float32) * gain
        vt[0:DH, span] = values.T.astype(jnp.bfloat16)
        vt[DH:VROWS, span] = jnp.where(row == 0, gain, 0.0).astype(jnp.bfloat16)

    for j in range(HEADS):
        logit = jnp.full((8, DH), gate_ref[j], jnp.float32)
        opening[:, j * DH : (j + 1) * DH] = 1.0 / (1.0 + jnp.exp(-logit))

    hop = (2, 1, -2, -1)

    def message(kind, p, r, step=None):
        to = plane(hop[kind] if step is None else step)
        return [
            pltpu.make_async_remote_copy(
                src_ref=src, dst_ref=dst, send_sem=send, recv_sem=recv, device_id=(to, h), device_id_type=MESH
            )
            for src, dst, send, recv in (
                (
                    out_s.at[kind, p, r, pl.ds(0, 2)],
                    in_s.at[kind, p, r, pl.ds(0, 2)],
                    s_send.at[kind, p, r],
                    s_recv.at[kind, p, r],
                ),
                (out_o.at[kind, p, r], in_o.at[kind, p, r], m_send.at[kind, p, r], m_recv.at[kind, p, r]),
            )
        ]

    def send(kind, p, r, part, step=None):
        out_o[kind, p, r] = part[0].astype(jnp.bfloat16)
        out_s[kind, p, r, 0:1] = part[1]
        out_s[kind, p, r, 1:2] = part[2]
        for copy in message(kind, p, r, step):
            copy.start()

    def receive(kind, p, r):
        for copy in message(kind, p, r):
            copy.wait_recv()
        return in_o[kind, p, r].astype(jnp.float32), in_s[kind, p, r, 0:1], in_s[kind, p, r, 1:2]

    units = (
        (0, 0), (0, 1), (0, 2), (1, 0), (1, 1), (2, 0), (1, 2), (3, 0),
        (2, 1), (3, 1), (0, 3), (2, 2), (3, 2), (1, 3), (2, 3), (3, 3),
    )

    def schedule(u):
        p = r = 0
        for a in range(1, len(units)):
            on = lax.div(u + (len(units) - a), len(units))
            p = p + (units[a][0] - units[a - 1][0]) * on
            r = r + (units[a][1] - units[a - 1][1]) * on
        return p, r

    def rows_of(p, step):
        return qa[p, pl.ds(pl.multiple_of(plane(step) * CHUNK, CHUNK), CHUNK), :]

    def unit_rows(u):
        p, r = schedule(u)
        own = (8 - 2 * r) * lax.div(r + 3, 4)
        steps = (8 - 2 * r, 7 - 2 * r, -own, 2 * r - 7)
        return jnp.concatenate([rows_of(p, step) for step in steps], axis=0)

    def score_tile(q, slot, k):
        s = lax.dot_general(
            kp[k : k + TILE, :], q, (((1,), (1,)), ((), ())), preferred_element_type=jnp.float32
        )
        scores[slot, k : k + TILE, :] = s
        return jnp.max(s.reshape(TILE // 8, 8, 4 * CHUNK), axis=0)

    def value_tile(slot, m, k):
        w = jnp.exp2((scores[slot, k : k + TILE, :] - m) * SCALE).astype(jnp.bfloat16)
        return jnp.dot(vt[:, k : k + TILE], w, preferred_element_type=jnp.float32)

    def unit(q_next, m, slot):
        top = acc = None
        for k in range(0, KEYS, TILE):
            t = score_tile(q_next, 1 - slot, k)
            top = t if top is None else jnp.maximum(top, t)
            acc = add(acc, value_tile(slot, m, k))
        return acc, jnp.max(top, axis=0, keepdims=True)

    left_lanes = lax.broadcasted_iota(jnp.int32, (DH // 2, FOLD), 1) < CHUNK
    left_line = lax.broadcasted_iota(jnp.int32, (8, FOLD), 1) < CHUNK

    def folded(acc, m, side):
        lanes = slice(side * FOLD, (side + 1) * FOLD)
        upper, lower = acc[0 : DH // 2, lanes], acc[DH // 2 : DH, lanes]
        even = [jnp.where(left_lanes, upper, pltpu.roll(lower, CHUNK, 1))]
        odd = [jnp.where(left_lanes, pltpu.roll(upper, CHUNK, 1), lower)]
        for line in (m[:, lanes], acc[DH : DH + 1, lanes]):
            line = jnp.broadcast_to(line, (8, FOLD))
            other = pltpu.roll(line, CHUNK, 1)
            even.append(jnp.where(left_line, line, other)[0:1])
            odd.append(jnp.where(left_line, other, line)[0:1])
        return even, odd

    wait_rows(0)
    q = unit_rows(0)
    top = None
    for k in range(0, KEYS, TILE):
        t = score_tile(q, 0, k)
        top = t if top is None else jnp.maximum(top, t)
    top = jnp.max(top, axis=0, keepdims=True)

    def keep(side, p, r, part):
        part_o[side, p, r] = part[0]
        part_s[side, p, r, 0:1] = part[1]
        part_s[side, p, r, 1:2] = part[2]

    def kept(side, p, r):
        return part_o[side, p, r], part_s[side, p, r, 0:1], part_s[side, p, r, 1:2]

    def pass_seven(p):
        send(1, p, 0, merge([kept(0, p, 0), receive(0, p, 0)]))

    def pass_on(p, r):
        for side in range(2):
            parts = [kept(side, p, r)]
            if r > 1 or (side == 0 and p > 1):
                parts.append(receive(2 * side, p, r - 1))
            parts.append(receive(2 * side + 1, p, r - 1))
            send(2 * side, p, r, merge(parts))

    def finish(u, acc, m):
        p, r = schedule(u)
        even, odd = folded(acc, m, 0)

        @pl.when(r == 0)
        def _():
            send(0, p, r, even, 1 + lax.div(p, 2))

        @pl.when(r > 0)
        def _():
            keep(0, p, r, even)

        waits = jnp.logical_and(r == 0, p < 2)

        @pl.when(waits)
        def _():
            keep(0, p, 0, odd)

        @pl.when(jnp.logical_not(waits))
        def _():
            send(1, p, r, odd)

        even, odd = folded(acc, m, 1)
        send(3, p, r, odd)
        keep(1, p, r, even)

    def body(i, m):
        for p in range(1, PHASES):

            @pl.when(i == p)
            def _():
                if p == 3:
                    pass_seven(1)
                wait_rows(p)

        acc, m_next = unit(unit_rows(2 * i + 1), m, 0)
        finish(2 * i, acc, m)
        acc, m = unit(unit_rows(2 * i + 2 - lax.div(i, 7)), m_next, 1)
        finish(2 * i + 1, acc, m_next)
        for at, hops in (
            (1, ((0, 0),)),
            (3, ((0, 1),)),
            (4, ((1, 1), (2, 1))),
            (5, ((0, 2), (3, 1))),
            (6, ((1, 2), (2, 2))),
        ):

            @pl.when(i == at)
            def _():
                for p, r in hops:
                    if r:
                        pass_on(p, r)
                    else:
                        pass_seven(p)

        return m

    lax.fori_loop(0, PHASES * ROUNDS // 2, body, top)

    def give_back(p):
        parts = [receive(kind, p, ROUNDS - 1) for kind in range(4)]
        parts.append(kept(1, p, 0))
        o, _, l = merge(parts)
        turned = jnp.concatenate([o / l] * 2, axis=0).T
        read = jnp.where(left_lanes, turned[0:CHUNK], turned[CHUNK:])
        result[p] = read.astype(jnp.bfloat16).astype(jnp.float32)

        def give(b, _):
            to = lax.div(b, 4) * 16 + 4 * p + lax.rem(b, 4)

            @pl.when(to != h)
            def _():
                pltpu.make_async_remote_copy(
                    src_ref=result.at[p, pl.ds(pl.multiple_of(b * 8, 8), 8), :],
                    dst_ref=read_ref.at[:, pl.ds(pl.multiple_of(h * DH, DH), DH)],
                    send_sem=r_send,
                    recv_sem=r_recv,
                    device_id=(g, to),
                    device_id_type=MESH,
                ).start()

            @pl.when(to == h)
            def _():
                read_ref[:, pl.ds(pl.multiple_of(h * DH, DH), DH)] = result[
                    p, pl.ds(pl.multiple_of(b * 8, 8), 8), :
                ]

            return 0

        lax.fori_loop(0, 8, give, 0)

    pass_on(0, 3)
    pass_on(3, 2)
    pass_on(1, 3)
    pass_on(2, 3)
    give_back(0)
    pass_on(3, 3)
    give_back(1)
    give_back(2)
    give_back(3)

    for p in range(PHASES):
        part = qa.at[p, pl.ds(0, (HEADS - 1) * PART), :]
        pltpu.make_async_copy(part, part, q_send.at[p]).wait()
        for kind in range(4):
            for r in range(ROUNDS):
                if kind == 2 and r == 0:
                    continue
                for copy in message(kind, p, r):
                    copy.wait_send()
    span = read_ref.at[:, pl.ds(0, (HEADS - 1) * DH)]
    pltpu.make_async_copy(span, span, r_send).wait()
    pltpu.make_async_copy(span, span, r_recv).wait()
    gate = opening[...]
    near = near_ref[...].astype(jnp.float32)
    mixed_ref[...] = (gate * read_ref[...] + (1.0 - gate) * near).astype(jnp.bfloat16)


def local(queries, local_read, gate_logits, memory_keys, memory_values, probe_blocks, probe_counts):
    vmem = pl.BlockSpec(memory_space=pltpu.VMEM)
    hbm = pl.BlockSpec(memory_space=pl.ANY)
    return pl.pallas_call(
        kernel,
        out_shape=jax.ShapeDtypeStruct((8, HEADS * DH), jnp.bfloat16),
        in_specs=[hbm] * 7,
        out_specs=vmem,
        scratch_shapes=[
            pltpu.SMEM((1, 1, PMAX), jnp.int32),
            pltpu.SMEM((1, 1), jnp.int32),
            pltpu.SMEM((HEADS,), jnp.float32),
            pltpu.VMEM((32, BLOCK, DH), jnp.bfloat16),
            pltpu.VMEM((32, BLOCK, DH), jnp.bfloat16),
            pltpu.VMEM((8, HEADS * DH), jnp.bfloat16),
            pltpu.VMEM((8, HEADS * DH), jnp.float32),
            pltpu.VMEM((8, HEADS * DH), jnp.float32),
            pltpu.VMEM((PHASES, HEADS * PART, DH), jnp.bfloat16),
            pltpu.VMEM((KEYS, DH), jnp.bfloat16),
            pltpu.VMEM((VROWS, KEYS), jnp.bfloat16),
            pltpu.VMEM((2, KEYS, 4 * CHUNK), jnp.float32),
            pltpu.VMEM((2, PHASES, ROUNDS, DH // 2, FOLD), jnp.float32),
            pltpu.VMEM((2, PHASES, ROUNDS, 8, FOLD), jnp.float32),
            pltpu.VMEM((4, PHASES, ROUNDS, DH // 2, FOLD), jnp.bfloat16),
            pltpu.VMEM((4, PHASES, ROUNDS, 8, FOLD), jnp.float32),
            pltpu.VMEM((4, PHASES, ROUNDS, DH // 2, FOLD), jnp.bfloat16),
            pltpu.VMEM((4, PHASES, ROUNDS, 8, FOLD), jnp.float32),
            pltpu.VMEM((PHASES, CHUNK, DH), jnp.float32),
            pltpu.SemaphoreType.DMA((PHASES + 6,)),
            pltpu.SemaphoreType.DMA((PHASES,)),
            pltpu.SemaphoreType.DMA((PHASES,)),
            pltpu.SemaphoreType.DMA((4, PHASES, ROUNDS)),
            pltpu.SemaphoreType.DMA((4, PHASES, ROUNDS)),
            pltpu.SemaphoreType.DMA((4, PHASES, ROUNDS)),
            pltpu.SemaphoreType.DMA((4, PHASES, ROUNDS)),
            pltpu.SemaphoreType.DMA,
            pltpu.SemaphoreType.DMA,
        ],
        compiler_params=pltpu.CompilerParams(
            collective_id=0, has_side_effects=True, vmem_limit_bytes=63 << 20
        ),
        name="memory_reads",
    )(
        probe_blocks,
        probe_counts,
        gate_logits,
        queries,
        memory_keys.reshape(-1, BLOCK, DH),
        memory_values.reshape(-1, BLOCK, DH),
        local_read,
    )


def solution(mesh):
    return jax.shard_map(
        local,
        mesh=mesh,
        in_specs=(
            P("head", None),
            P(("index", "head"), None),
            P(),
            P("index", "head", None, None),
            P("index", "head", None, None),
            P("index", "head", None),
            P("index", "head"),
        ),
        out_specs=P(("index", "head"), None),
        check_vma=False,
    )
```
